32 devices in a mesh: section: 2 (over x), expert: 4 (over y, core), dp: 4 (over z).
Axes of the slice: x: 2, y: 2, z: 4, core: 2. Of those that a mesh axis runs over, the one named last changes fastest.
Arguments:
- tokens: bfloat16 [512, 3072], P('expert', 'dp'), may hold values from -6 to 6
- expert_ids: int32 [512, 2], P('expert'), may hold values from 0 to 3, all different within a row; in each aligned block of 128 rows (0 to 127, 128 to 255, ...) at most 128 rows name the same one
- w_gate: bfloat16 [4, 3072, 8192], P('expert', 'dp', 'section'), may hold values from -0.109375 to 0.109375
- w_up: bfloat16 [4, 3072, 8192], P('expert', 'dp', 'section'), may hold values from -0.109375 to 0.109375
- cotangent: bfloat16 [4, 512, 8192], P('expert', None, 'section'), may hold values from -6 to 6
Outputs:
- acted: bfloat16 [4, 512, 8192], P('expert', None, 'section')
- input_grad: bfloat16 [512, 3072], P('expert', 'dp')
- gate_grad: bfloat16 [4, 3072, 8192], P('expert', 'dp', 'section')
- up_grad: bfloat16 [4, 3072, 8192], P('expert', 'dp', 'section')
The draws below stay inside these ranges and needn't reach their ends.
Inputs may be any that keep to these rules, and one draw needn't show every extreme that they name: `expert_ids`: each token names two different experts. Among the 128 tokens of one index of the expert axis no expert is named more than 128 times, a bound that some block reaches.
All inputs are finite; a program needn't handle non-finite values.
Results may differ from the reference program's by a relative error of at most 0.0049.
Values may be sent and summed in bfloat16 or wider, within the bound.
No kernel may reach another device: no remote copies, remote signals or barrier semaphores. Data moves between devices by JAX's collectives and lax.ppermute only.
A program may use at most 128 MiB of HBM per device.

```python
import math
import jax
import jax.numpy as jnp
import numpy as np
from jax import lax

D = 3072
FF = 8192
TOK_DEV = 128
EXPERTS = 4
TOKENS = 512
CAP = 128
SLOTS = 512
N_EXPERT = 4


def level_of(key, shape, pieces, least, largest):
    loudness, own = 1.0, jax.random.fold_in(key, 6)
    for dim, parts in pieces:
        heights = jnp.exp(jax.random.uniform(jax.random.fold_in(own, dim), (parts,), jnp.float32, least / len(pieces), largest / len(pieces)))
        loudness = loudness * jnp.repeat(heights, shape[dim] // parts).reshape([-1 if axis == dim else 1 for axis in range(len(shape))])
    return loudness


def deal_out(rng, own, number, rows, count, top, limit, slope):
    ranking = jax.random.permutation(rng, count)
    heavy_load, common = shares(count, rows * top, limit, slope, True), shares(count, rows * top, limit, slope, False)
    places = jnp.arange(count)

    def named(lengths, offset_by):
        used = int((lengths > 0).sum())
        fixed = max(1, used // 4)
        passed = fixed + (places - fixed + offset_by * (used - fixed)) % max(1, count - fixed)
        return jnp.zeros((count,), jnp.int32).at[ranking[jnp.where(places < fixed, places, passed)]].set(jnp.asarray(lengths, jnp.int32))

    lengths = jnp.where(number % 4 == 0, named(heavy_load, number // 4), named(common, number - number // 4 - 1))
    mixed = jax.random.permutation(jax.random.fold_in(own, 3), count)
    source_of, receiver = mixed[0:count // 2 * 2:2], mixed[1:count // 2 * 2:2]
    margin = jnp.minimum(lengths[source_of] - 1, limit - lengths[receiver]) // 2
    margin = jnp.where((source_of == ranking[0]) | (receiver == ranking[0]) | (lengths[receiver] == 0), 0, jnp.maximum(margin, 0))
    passed = jax.random.randint(jax.random.fold_in(own, 4), (count // 2,), 0, 1 << 20) % (margin + 1)
    lengths = lengths.at[source_of].add(-passed).at[receiver].add(passed)
    items = jnp.searchsorted(jnp.cumsum(lengths), jnp.arange(rows * top), side="right").astype(jnp.int32)
    table = items.reshape(top, rows).T
    table = table[jax.random.permutation(jax.random.fold_in(own, 1), rows)]
    offset_by = jax.random.randint(jax.random.fold_in(own, 2), (rows, 1), 0, top)
    return jnp.take_along_axis(table, (jnp.arange(top)[None, :] + offset_by) % top, axis=1)


def shares(count, total, most, skew, full):
    loads = [(1 << 20) // math.isqrt(grade ** skew) + 1 for grade in range(1, count + 1)]
    largest = most if full else min(most, max(-(-total // count), total * loads[0] // sum(loads)))
    least = 1 if total - largest >= count - 1 else 0
    counts, rest = [largest] + [least] * (count - 1), total - largest - least * (count - 1)
    while rest > 0:
        movable = [i for i in range(1, count) if counts[i] < largest] or [i for i in range(1, count) if counts[i] < most]
        pool, left = sum([loads[i] for i in movable]), rest
        for i in movable:
            addition = min(most - counts[i], max(1, left * loads[i] // pool), rest)
            counts[i] = counts[i] + addition
            rest = rest - addition
    return np.array(counts)


def centred(own_key, extent, scale, most, cuts=(), kind=jnp.bfloat16):
    result = jax.random.normal(own_key, extent, jnp.float32) * scale
    if len(cuts) > 0:
        result = level_of(own_key, extent, cuts, -0.22, 0.18) * result
    return jnp.clip(result, min=-most, max=most).astype(kind)


def setup_inputs(seed: int = 0) -> dict:
    streams_of = jax.random.split(jax.random.key(seed), 6)
    tokens = centred(streams_of[0], (TOKENS, D), 1.0, 6.0, ((0, 4), (1, 4)))
    expert_ids_keys = jax.random.split(jax.random.fold_in(streams_of[1], 1), TOKENS // TOK_DEV)
    expert_ids_turns = jax.random.permutation(jax.random.fold_in(streams_of[1], 3), TOKENS // TOK_DEV)
    expert_ids = jax.vmap(lambda own, number: deal_out(jax.random.fold_in(streams_of[1], 2), own, number, TOK_DEV, EXPERTS, 2, CAP, 2))(expert_ids_keys, expert_ids_turns).reshape((TOKENS, 2))
    w_gate = centred(streams_of[2], (EXPERTS, D, FF), D ** -0.5, 0.109375, ((0, 4), (1, 4), (2, 2)))
    w_up = centred(streams_of[3], (EXPERTS, D, FF), D ** -0.5, 0.109375, ((0, 4), (1, 4), (2, 2)))
    cotangent = centred(streams_of[4], (EXPERTS, SLOTS, FF), 1.0, 6.0, ((0, 4), (2, 2)))
    return dict(tokens=tokens, expert_ids=expert_ids, w_gate=w_gate, w_up=w_up, cotangent=cotangent)


def expert_slots(ids, which):
    hits = (ids == which).reshape(N_EXPERT, 2 * TOK_DEV).astype(jnp.int32)
    rank = jnp.cumsum(hits, axis=1) - hits
    group = jnp.arange(N_EXPERT, dtype=jnp.int32)[:, None]
    slot = jnp.where(hits > 0, group * CAP + rank, N_EXPERT * CAP).astype(jnp.int32)
    token = (jnp.arange(TOKENS * 2, dtype=jnp.int32) // 2).reshape(N_EXPERT, 2 * TOK_DEV)
    source = jnp.full((N_EXPERT * CAP,), TOKENS, jnp.int32).at[slot.reshape(-1)].set(
        token.reshape(-1), mode="drop")
    return slot.reshape(-1), source


def reference(tokens, expert_ids, w_gate, w_up, cotangent):
    x_pad = jnp.concatenate([tokens, jnp.zeros((1, D), jnp.bfloat16)], axis=0)

    def per_expert(carry, item):
        which, wg, wu, cot = item
        slot, source = expert_slots(expert_ids, which)
        rows = jnp.take(x_pad, source, axis=0)
        pre_gate = jnp.dot(rows, wg, preferred_element_type=jnp.float32)
        pre_up = jnp.dot(rows, wu, preferred_element_type=jnp.float32)
        sig = jax.nn.sigmoid(pre_gate)
        silu_v = pre_gate * sig
        acted = (silu_v * pre_up).astype(jnp.bfloat16)
        cf = cot.astype(jnp.float32)
        gate_part = (cf * pre_up * sig * (1.0 + pre_gate * (1.0 - sig))).astype(jnp.bfloat16)
        up_part = (cf * silu_v).astype(jnp.bfloat16)
        gate_grad = jnp.dot(rows.T, gate_part, preferred_element_type=jnp.float32).astype(jnp.bfloat16)
        up_grad = jnp.dot(rows.T, up_part, preferred_element_type=jnp.float32).astype(jnp.bfloat16)
        back = (jnp.dot(gate_part, wg.T, preferred_element_type=jnp.float32)
                + jnp.dot(up_part, wu.T, preferred_element_type=jnp.float32))
        back_pad = jnp.concatenate([back, jnp.zeros((1, D), jnp.float32)], axis=0)
        per_token = jnp.take(back_pad, slot, axis=0).reshape(TOKENS, 2, D)
        carry = carry + jnp.sum(per_token, axis=1)
        return carry, (acted, gate_grad, up_grad)

    numbers = jnp.arange(EXPERTS).astype(jnp.int32)
    start = jnp.zeros((TOKENS, D), jnp.float32)
    total, outs = lax.scan(per_expert, start, (numbers, w_gate, w_up, cotangent))
    return (outs[0], total.astype(jnp.bfloat16), outs[1], outs[2])
```

```python
import functools

import jax
import jax.numpy as jnp
from jax import lax
from jax.experimental import pallas as pl
from jax.experimental.pallas import tpu as pltpu
from jax.sharding import PartitionSpec as P

BF, HALF, F32 = jnp.bfloat16, jnp.float16, jnp.float32
SCALE = 16.0
OUT, MID, BACK = [(0, 1), (3, 2)], [(1, 2), (2, 1)], [(1, 0), (2, 3)]
MIB = 1024 * 1024


def dot(a, b, dims=((1,), (0,))):
    return lax.dot_general(a, b, (dims, ((), ())), preferred_element_type=F32)


def swap(value, axis, stride):
    n = lax.axis_size(axis)
    return lax.ppermute(value, axis, [(i, i ^ stride) for i in range(n)])


def gather_expert(value):
    n = lax.axis_size("expert")
    me = lax.axis_index("expert")
    held, stage, stride = value, 0, n // 2
    while stride >= 1:
        other = swap(held, "expert", stride)
        low = (me & stride) == 0
        held = jnp.stack([jnp.where(low, held, other), jnp.where(low, other, held)], axis=stage)
        stage, stride = stage + 1, stride // 2
    return held.reshape((n,) + value.shape)


def scatter_expert(value):
    n = lax.axis_size("expert")
    me = lax.axis_index("expert")
    stride = 1
    while stride < n:
        value = value.reshape((-1, 2) + value.shape[1:])
        low = (me & stride) == 0
        keep = jnp.where(low, value[:, 0], value[:, 1])
        send = jnp.where(low, value[:, 1], value[:, 0])
        got = swap(send, "expert", stride)
        value = (keep.astype(F32) + got.astype(F32)).astype(BF)
        stride *= 2
    return value[0]


def chunks_of(total):
    body, ramp = 512, [256, 256]
    while ramp and total < 2 * sum(ramp) + body:
        body = ramp.pop()
    count, rest = divmod(total - 2 * sum(ramp), body)
    assert rest == 0 and count > 0
    at = 0
    for size in ramp + [body] * count + ramp[::-1]:
        yield at, size
        at += size


ANY = pl.BlockSpec(memory_space=pl.ANY)
TOKEN = jax.ShapeDtypeStruct((8, 128), F32)


def whole(shape):
    return pl.BlockSpec(shape, lambda i: (0,) * len(shape))


class Part:
    def __init__(self, at, n):
        self.at, self.n, self.wide = at, n, min(n, 256)
        self.steps = n // self.wide

    def inside(self, height):
        first, steps = self.at // self.wide, self.steps
        return pl.BlockSpec((height, self.wide), lambda i: (0, first + jnp.minimum(i, steps - 1)))

    def own(self, height):
        steps = self.steps
        return pl.BlockSpec((height, 2 * self.wide), lambda i: (0, jnp.minimum(i, steps - 1)))


def call(body, steps, ins, in_specs, outs, out_specs, alias, vmem):
    return pl.pallas_call(
        body,
        grid=(steps,),
        in_specs=in_specs,
        out_specs=out_specs,
        out_shape=outs,
        input_output_aliases=alias,
        compiler_params=pltpu.CompilerParams(vmem_limit_bytes=vmem),
        cost_estimate=pl.CostEstimate(flops=1, bytes_accessed=1, transcendentals=0),
    )(*ins)


def produce_body(x_ref, wg_ref, wu_ref, p_ref):
    n = wg_ref.shape[1]
    p_ref[:, :n] = dot(x_ref[...], wg_ref[...])
    p_ref[:, n:] = dot(x_ref[...], wu_ref[...])


def finish_body(first, x_ref, wg_ref, wu_ref, t_ref, pick_ref, cot_ref, back_in, acted_ref, gg_ref, ug_ref, back_ref):
    n = wg_ref.shape[1]

    @pl.when(first)
    def _():
        back_ref[...] = back_in[...]

    pre_gate, pre_up = t_ref[:, :n], t_ref[:, n:]
    sig = jax.nn.sigmoid(pre_gate)
    silu_v = pre_gate * sig
    cf = dot(pick_ref[...], cot_ref[...])
    gp = (cf * pre_up * sig * (1.0 + pre_gate * (1.0 - sig))).astype(BF)
    up = (cf * silu_v).astype(BF)
    acted = (silu_v * pre_up).astype(BF)
    acted_ref[...] = dot(pick_ref[...], acted, ((0,), (0,))).astype(BF)
    gg_ref[...] = dot(x_ref[...], gp, ((0,), (0,))).astype(BF)
    ug_ref[...] = dot(x_ref[...], up, ((0,), (0,))).astype(BF)
    back_ref[...] += dot(gp, wg_ref[...], ((1,), (1,))) + dot(up, wu_ref[...], ((1,), (1,)))


def main_call(token, x, wg, wu, make=None, end=None):
    rows, width = x.shape
    ins, in_specs = [token, x], [ANY, whole(x.shape)]
    outs, out_specs, alias = [TOKEN], [whole((8, 128))], {}
    end_steps = make_steps = 0
    if end is not None:
        part, t, pick, cot, acted, gg, ug, back = end
        end_steps = part.steps
        for arr, spec, into in (
            (wg, part.inside(width), None),
            (wu, part.inside(width), None),
            (t, part.own(rows), None),
            (pick, whole(pick.shape), None),
            (cot, part.inside(cot.shape[0]), None),
            (back, whole(back.shape), 4),
            (acted, ANY, 1),
            (gg, ANY, 2),
            (ug, ANY, 3),
        ):
            if arr is None:
                continue
            if into is not None:
                alias[len(ins)] = into
            ins.append(arr)
            in_specs.append(spec)
        outs += [jax.ShapeDtypeStruct(v, BF) for v in (cot.shape, wg.shape, wg.shape)]
        outs += [jax.ShapeDtypeStruct(back.shape, F32)]
        out_specs += [part.inside(cot.shape[0]), part.inside(width), part.inside(width), whole(back.shape)]
    if make is not None:
        make_steps, n = make.steps, make.n
        ins += [wg, wu]
        in_specs += [make.inside(width)] * 2
        outs.append(jax.ShapeDtypeStruct((rows, 2 * n), F32))
        out_specs.append(make.own(rows))
    n_in = len(ins)

    def body(*refs):
        i, o = refs[:n_in], refs[n_in:]
        step = pl.program_id(0)
        o[0][...] = jnp.zeros((8, 128), F32)
        if make is not None:

            @pl.when(step < make_steps)
            def _():
                produce_body(i[1], i[-2], i[-1], o[-1])

        if end is not None:

            @pl.when(step < end_steps)
            def _():
                finish_body(step == 0, *i[1:8], *o[1:5])

    return call(body, max(end_steps, make_steps), ins, in_specs, outs, out_specs, alias, 30 * MIB)


def pipeline(rows, cap, tokens, hit, rank, wg, wu, cot):
    groups, per = hit.shape
    width, hidden = wg.shape
    count = jnp.sum(hit.astype(F32), axis=1)
    first = jnp.cumsum(count) - count
    place = jnp.where(hit, first[:, None] + rank, -1.0).reshape(1, groups * per)
    row = jnp.arange(rows, dtype=F32)[:, None]
    take = (row == place).astype(BF)
    slot = jnp.arange(cap, dtype=F32)[None, :]
    slot_row = jnp.where(slot < count[:, None], first[:, None] + slot, -1.0).reshape(1, groups * cap)
    pick = (row == slot_row).astype(BF)
    x = dot(take, tokens).astype(BF)

    dp = lax.axis_index("dp")
    inner = (dp == 1) | (dp == 2)
    parts = [Part(at, n) for at, n in chunks_of(hidden)]
    acted = gg = ug = None
    back = jnp.zeros((rows, width), F32)
    token = jnp.zeros((8, 128), F32)
    p, a, q, b, t, c = {}, {}, {}, {}, {}, {}
    last = len(parts)

    def main(make, end):
        nonlocal token, acted, gg, ug, back
        done = end >= 0
        args = None
        if done:
            both = jnp.where(inner, t.pop(end), c.pop(end)).astype(F32) * (1.0 / SCALE)
            args = (parts[end], both, pick, cot, acted, gg, ug, back)
        out = main_call(token, x, wg, wu, parts[make] if make < last else None, args)
        token = out[0]
        if done:
            acted, gg, ug, back = out[1:5]
        if make < last:
            p[make] = out[-1] * SCALE
            a[make] = lax.ppermute(p[make].astype(HALF), "dp", OUT)

    main(0, -1)
    main(1, -1)
    for k in range(last + 2):
        if k < last:
            q[k] = (p.pop(k) + a.pop(k).astype(F32) + token[0, 0]).astype(HALF)
            b[k] = lax.ppermute(q[k], "dp", MID)
        if 1 <= k <= last:
            t[k - 1] = (q.pop(k - 1).astype(F32) + b.pop(k - 1).astype(F32) + token[0, 0]).astype(HALF)
            c[k - 1] = lax.ppermute(t[k - 1], "dp", BACK)
        after = [v[:8, :128].astype(F32) for v in (q.get(k), t.get(k - 1)) if v is not None]
        if after:
            token = sum(after)
        if k >= 2 or k + 2 < last:
            main(k + 2, k - 2)
    own = dot(take, back.astype(BF), ((0,), (0,))).astype(BF)
    return acted, gg, ug, own


def local(tokens, expert_ids, w_gate, w_up, cotangent):
    rows, width = tokens.shape
    experts = lax.axis_size("expert")
    cap = min(rows, 4 * rows // experts)
    wg, wu, cot = w_gate[0], w_up[0], cotangent[0]
    me = lax.axis_index("expert")
    ids = jnp.pad(expert_ids.astype(BF), ((0, 0), (0, 126)))
    held = gather_expert(jnp.concatenate([tokens, ids], axis=1))
    all_tokens, all_ids = held[:, :, :width], held[:, :, width : width + 2]
    hit = jnp.any(all_ids == me.astype(BF), axis=2)
    before = (jnp.arange(rows)[:, None] < jnp.arange(rows)[None, :]).astype(BF)
    rank = dot(hit.astype(BF), before)
    slots = experts * cap
    sizes = sorted({slots * part // 16 for part in (4, 6, 8, 12, 16)})
    filled = jnp.sum(hit.astype(jnp.int32))
    which = jnp.sum((filled > jnp.array(sizes[:-1], jnp.int32)).astype(jnp.int32))
    acted, gg, ug, own = lax.switch(
        which,
        [functools.partial(pipeline, size, cap) for size in sizes],
        all_tokens.reshape(experts * rows, width),
        hit,
        rank,
        wg,
        wu,
        cot,
    )
    part = scatter_expert(own.reshape(experts, rows, width))
    if lax.axis_size("section") == 2:
        total = part.astype(F32) + swap(part, "section", 1).astype(F32)
    else:
        total = lax.psum(part.astype(F32), "section")
    return acted[None], total.astype(BF), gg[None], ug[None]


def solution(mesh):
    placed = (
        P("expert", "dp"),
        P("expert", None),
        P("expert", "dp", "section"),
        P("expert", "dp", "section"),
        P("expert", None, "section"),
    )
    return jax.shard_map(
        local,
        mesh=mesh,
        in_specs=placed,
        out_specs=(
            P("expert", None, "section"),
            P("expert", "dp"),
            P("expert", "dp", "section"),
            P("expert", "dp", "section"),
        ),
        check_vma=False,
    )
```

```python
import functools
import math

import jax
import jax.numpy as jnp
from jax import lax
from jax.experimental import pallas as pl
from jax.experimental.pallas import tpu as pltpu
from jax.sharding import PartitionSpec as P

BF, HALF, F32 = jnp.bfloat16, jnp.float16, jnp.float32
DONE = 3
BODY = 384
OUT, MID, BACK = [(0, 1), (3, 2)], [(1, 2), (2, 1)], [(1, 0), (2, 3)]
MIB = 1024 * 1024


def dot(a, b, dims=((1,), (0,))):
    return lax.dot_general(a, b, (dims, ((), ())), preferred_element_type=F32)


def then(value, after):
    return lax.optimization_barrier((value, after))[0]


def swap(value, axis, stride):
    n = lax.axis_size(axis)
    return lax.ppermute(value, axis, [(i, i ^ stride) for i in range(n)])


def gather_expert(value):
    n = lax.axis_size("expert")
    me = lax.axis_index("expert")
    held, stage, stride = value, 0, n // 2
    while stride >= 1:
        other = swap(held, "expert", stride)
        low = (me & stride) == 0
        held = jnp.stack([jnp.where(low, held, other), jnp.where(low, other, held)], axis=stage)
        stage, stride = stage + 1, stride // 2
    return held.reshape((n,) + value.shape)


def scatter_expert(value):
    n = lax.axis_size("expert")
    me = lax.axis_index("expert")
    stride = 1
    while stride < n:
        value = value.reshape((-1, 2) + value.shape[1:])
        low = (me & stride) == 0
        keep = jnp.where(low, value[:, 0], value[:, 1])
        send = jnp.where(low, value[:, 1], value[:, 0])
        got = swap(send, "expert", stride)
        value = (keep.astype(F32) + got.astype(F32)).astype(BF)
        stride *= 2
    return value[0]


def chunks_of(total, body):
    body = min(body, total // 2)
    sizes = [body] * (total // body) + ([total % body] if total % body else [])
    return [(sum(sizes[:i]), n) for i, n in enumerate(sizes)]


ANY = pl.BlockSpec(memory_space=pl.ANY)


def whole(shape):
    return pl.BlockSpec(shape, lambda i: (0,) * len(shape))


class Part:
    def __init__(self, at, n):
        self.at, self.n, self.wide = at, n, n if n % 256 else 256
        self.steps = n // self.wide

    def inside(self, height):
        first, steps = self.at // self.wide, self.steps
        return pl.BlockSpec((height, self.wide), lambda i: (0, first + jnp.minimum(i, steps - 1)))

    def own(self, height):
        steps = self.steps
        return pl.BlockSpec((height, 2 * self.wide), lambda i: (0, jnp.minimum(i, steps - 1)))


def call(body, steps, ins, in_specs, outs, out_specs, alias, scratch, vmem):
    return pl.pallas_call(
        body,
        grid=(steps,),
        in_specs=in_specs,
        out_specs=out_specs,
        out_shape=outs,
        scratch_shapes=scratch,
        input_output_aliases=alias,
        compiler_params=pltpu.CompilerParams(vmem_limit_bytes=vmem),
        cost_estimate=pl.CostEstimate(flops=1, bytes_accessed=1, transcendentals=0),
    )(*ins)


def produce_body(x_ref, wg_ref, wu_ref, p_ref):
    n = wg_ref.shape[1]
    p_ref[:, :n] = dot(x_ref[...], wg_ref[...])
    p_ref[:, n:] = dot(x_ref[...], wu_ref[...])


def finish_body(first, packed, x_ref, wg_ref, wu_ref, t_ref, *refs):
    n = wg_ref.shape[1]
    pick_ref = refs[0] if packed else None
    cot_ref, back_in = refs[packed : packed + 2]
    acted_ref, gg_ref, ug_ref, back_ref = refs[-4:]

    @pl.when(first)
    def _():
        back_ref[...] = back_in[...]

    pre_gate, pre_up = t_ref[:, :n], t_ref[:, n:]
    sig = jax.nn.sigmoid(pre_gate)
    silu_v = pre_gate * sig
    cf = dot(pick_ref[...], cot_ref[...]) if packed else cot_ref[...].astype(F32)
    gp = (cf * pre_up * sig * (1.0 + pre_gate * (1.0 - sig))).astype(BF)
    up = (cf * silu_v).astype(BF)
    acted = (silu_v * pre_up).astype(BF)
    acted_ref[...] = dot(pick_ref[...], acted, ((0,), (0,))).astype(BF) if packed else acted
    gg_ref[...] = dot(x_ref[...], gp, ((0,), (0,))).astype(BF)
    ug_ref[...] = dot(x_ref[...], up, ((0,), (0,))).astype(BF)
    back_ref[...] += dot(gp, wg_ref[...], ((1,), (1,))) + dot(up, wu_ref[...], ((1,), (1,)))


def main_call(x, wg, wu, make=None, end=None):
    rows, width = x.shape
    ins, in_specs = [x], [whole(x.shape)]
    outs, out_specs, alias, scratch = [], [], {}, []
    end_steps = make_steps = 0
    if end is not None:
        part, t, pick, cot, acted, gg, ug, back = end
        packed = int(pick is not None)
        end_steps = part.steps
        for arr, spec, into in (
            (wg, part.inside(width), None),
            (wu, part.inside(width), None),
            (t, part.own(rows), None),
            (pick, None if pick is None else whole(pick.shape), None),
            (cot, part.inside(cot.shape[0]), None),
            (back, whole(back.shape), 3),
            (acted, ANY, 0),
            (gg, ANY, 1),
            (ug, ANY, 2),
        ):
            if arr is None:
                continue
            if into is not None:
                alias[len(ins)] = into
            ins.append(arr)
            in_specs.append(spec)
        outs += [jax.ShapeDtypeStruct(v, BF) for v in (cot.shape, wg.shape, wg.shape)]
        outs += [jax.ShapeDtypeStruct(back.shape, F32)]
        out_specs += [part.inside(cot.shape[0]), part.inside(width), part.inside(width), whole(back.shape)]
    if make is not None:
        make_steps, n = make.steps, make.n
        ins += [wg, wu]
        in_specs += [make.inside(width)] * 2
        outs.append(jax.ShapeDtypeStruct((rows, 2 * n), F32))
        out_specs.append(make.own(rows))
    n_in = len(ins)

    def body(*refs):
        i, o = refs[:n_in], refs[n_in:]
        step = pl.program_id(0)
        if make is not None:

            @pl.when(step < make_steps)
            def _():
                produce_body(i[0], i[-2], i[-1], o[-1])

        if end is not None:

            @pl.when(step < end_steps)
            def _():
                finish_body(step == 0, packed, *i[: 6 + packed], *o[:4])

    return call(body, max(end_steps, make_steps), ins, in_specs, outs, out_specs, alias, scratch, 30 * MIB)


def pipeline(rows, cap, scale, tokens, hit, rank, wg, wu, cot):
    groups, per = hit.shape
    width, hidden = wg.shape
    count = jnp.sum(hit.astype(F32), axis=1)
    packed = rows < groups * cap
    first = jnp.cumsum(count) - count if packed else cap * jnp.arange(groups, dtype=F32)
    place = jnp.where(hit, first[:, None] + rank, -1.0).reshape(1, groups * per)
    row = jnp.arange(rows, dtype=F32)[:, None]
    take = (row == place).astype(BF)
    x = dot(take, tokens).astype(BF)
    pick = None
    if packed:
        slot = jnp.arange(cap, dtype=F32)[None, :]
        slot_row = jnp.where(slot < count[:, None], first[:, None] + slot, -1.0).reshape(1, groups * cap)
        pick = (row == slot_row).astype(BF)

    dp = lax.axis_index("dp")
    inner = (dp == 1) | (dp == 2)
    parts = [Part(at, n) for at, n in chunks_of(hidden, BODY if 2 * rows > groups * cap else 1024)]
    acted = gg = ug = None
    back = jnp.zeros((rows, width), F32)
    token = x
    p, a, q, b, t, c = {}, {}, {}, {}, {}, {}
    last = len(parts)

    def finish(j):
        nonlocal token, acted, gg, ug, back
        both = jnp.where(inner, t.pop(j), c.pop(j)).astype(F32) * (1.0 / scale)
        args = (parts[j], both, pick, cot, acted, gg, ug, back)
        acted, gg, ug, back = main_call(then(x, token), wg, wu, None, args)
        token = back

    def add(one, two):
        return (one.astype(F32) + two.astype(F32)).astype(HALF)

    def make(j):
        p[j] = (main_call(then(x, token), wg, wu, parts[j])[0] * scale).astype(HALF)

    def send(j):
        a[j] = lax.ppermute(then(p[j], token), "dp", OUT)

    for j in range(min(2, last)):
        make(j)
        send(j)
    for j in range(2, min(4, last)):
        make(j)
    for k in range(last + DONE):
        if k < last:
            q[k] = token = add(p.pop(k), then(a.pop(k), token))
            b[k] = lax.ppermute(q[k], "dp", MID)
        if k + 2 < last:
            send(k + 2)
        if 0 <= k - 1 < last:
            t[k - 1] = token = add(q.pop(k - 1), then(b.pop(k - 1), token))
            c[k - 1] = lax.ppermute(t[k - 1], "dp", BACK)
        for j in (2 * k + 4, 2 * k + 5):
            if j < last:
                make(j)
        if k >= DONE:
            finish(k - DONE)
    own = dot(take, back.astype(BF), ((0,), (0,))).astype(BF)
    return acted, gg, ug, own


def local(tokens, expert_ids, w_gate, w_up, cotangent):
    rows, width = tokens.shape
    experts = lax.axis_size("expert")
    cap = min(rows, 4 * rows // experts)
    wg, wu, cot = w_gate[0], w_up[0], cotangent[0]
    me = lax.axis_index("expert")
    bound = 6.0 * 0.109375 * width * lax.axis_size("dp")
    scale = 2.0 ** math.floor(math.log2(65000.0 / bound))
    ids = jnp.pad(expert_ids.astype(BF), ((0, 0), (0, 126)))
    held = gather_expert(jnp.concatenate([tokens, ids], axis=1))
    all_tokens, all_ids = held[:, :, :width], held[:, :, width : width + 2]
    hit = jnp.any(all_ids == me.astype(BF), axis=2)
    before = (jnp.arange(rows)[:, None] < jnp.arange(rows)[None, :]).astype(BF)
    rank = dot(hit.astype(BF), before)
    slots = experts * cap
    sizes = sorted({slots * part // 16 for part in (6, 8, 16)}, reverse=True)
    filled = jnp.sum(hit.astype(jnp.int32))
    which = jnp.sum((filled <= jnp.array(sizes[1:], jnp.int32)).astype(jnp.int32))
    acted, gg, ug, own = lax.switch(
        which,
        [functools.partial(pipeline, size, cap, scale) for size in sizes],
        all_tokens.reshape(experts * rows, width),
        hit,
        rank,
        wg,
        wu,
        cot,
    )
    part = scatter_expert(own.reshape(experts, rows, width))
    if lax.axis_size("section") == 2:
        total = part.astype(F32) + swap(part, "section", 1).astype(F32)
    else:
        total = lax.psum(part.astype(F32), "section")
    return acted[None], total.astype(BF), gg[None], ug[None]


def solution(mesh):
    placed = (
        P("expert", "dp"),
        P("expert", None),
        P("expert", "dp", "section"),
        P("expert", "dp", "section"),
        P("expert", None, "section"),
    )
    return jax.shard_map(
        local,
        mesh=mesh,
        in_specs=placed,
        out_specs=(
            P("expert", None, "section"),
            P("expert", "dp"),
            P("expert", "dp", "section"),
            P("expert", "dp", "section"),
        ),
        check_vma=False,
    )
```

```python
import functools
import math

import jax
import jax.numpy as jnp
from jax import lax
from jax.experimental import pallas as pl
from jax.experimental.pallas import tpu as pltpu
from jax.sharding import PartitionSpec as P

BF, HALF, F32 = jnp.bfloat16, jnp.float16, jnp.float32
BODY, LAG = 256, 3
LIGHT_BODY, LIGHT_LAG = 512, 2
SIDE, MID = [(0, 1), (1, 0), (2, 3), (3, 2)], [(1, 2), (2, 1)]
MIB = 1024 * 1024


def dot(a, b, dims=((1,), (0,))):
    return lax.dot_general(a, b, (dims, ((), ())), preferred_element_type=F32)


def then(value, after):
    return lax.optimization_barrier((value, after))[0]


def swap(value, axis, stride):
    n = lax.axis_size(axis)
    return lax.ppermute(value, axis, [(i, i ^ stride) for i in range(n)])


def gather_expert(value):
    n = lax.axis_size("expert")
    me = lax.axis_index("expert")
    held, stage, stride = value, 0, n // 2
    while stride >= 1:
        other = swap(held, "expert", stride)
        low = (me & stride) == 0
        held = jnp.stack([jnp.where(low, held, other), jnp.where(low, other, held)], axis=stage)
        stage, stride = stage + 1, stride // 2
    return held.reshape((n,) + value.shape)


def scatter_expert(value):
    n = lax.axis_size("expert")
    me = lax.axis_index("expert")
    stride = 1
    while stride < n:
        value = value.reshape((-1, 2) + value.shape[1:])
        low = (me & stride) == 0
        keep = jnp.where(low, value[:, 0], value[:, 1])
        send = jnp.where(low, value[:, 1], value[:, 0])
        got = swap(send, "expert", stride)
        value = (keep.astype(F32) + got.astype(F32)).astype(BF)
        stride *= 2
    return value[0]


def chunks_of(total, body):
    body = min(body, total // 2)
    sizes = [body] * (total // body) + ([total % body] if total % body else [])
    return [(sum(sizes[:i]), n) for i, n in enumerate(sizes)]


ANY = pl.BlockSpec(memory_space=pl.ANY)


def whole(shape):
    return pl.BlockSpec(shape, lambda i: (0,) * len(shape))


class Part:
    def __init__(self, at, n):
        self.at, self.n, self.wide = at, n, n if n % 256 else 256
        self.steps = n // self.wide

    def inside(self, height):
        first, steps = self.at // self.wide, self.steps
        return pl.BlockSpec((height, self.wide), lambda i: (0, first + jnp.minimum(i, steps - 1)))

    def own(self, height):
        steps = self.steps
        return pl.BlockSpec((height, 2 * self.wide), lambda i: (0, jnp.minimum(i, steps - 1)))


def call(body, steps, ins, in_specs, outs, out_specs, alias, scratch, vmem):
    return pl.pallas_call(
        body,
        grid=(steps,),
        in_specs=in_specs,
        out_specs=out_specs,
        out_shape=outs,
        scratch_shapes=scratch,
        input_output_aliases=alias,
        compiler_params=pltpu.CompilerParams(vmem_limit_bytes=vmem),
        cost_estimate=pl.CostEstimate(flops=1, bytes_accessed=1, transcendentals=0),
    )(*ins)


def produce_body(x_ref, wg_ref, wu_ref, p_ref):
    n = wg_ref.shape[1]
    p_ref[:, :n] = dot(x_ref[...], wg_ref[...])
    p_ref[:, n:] = dot(x_ref[...], wu_ref[...])


def finish_body(first, packed, x_ref, wg_ref, wu_ref, t_ref, *refs):
    n = wg_ref.shape[1]
    pick_ref = refs[0] if packed else None
    cot_ref, back_in = refs[packed : packed + 2]
    acted_ref, gg_ref, ug_ref, back_ref = refs[-4:]

    @pl.when(first)
    def _():
        back_ref[...] = back_in[...]

    pre_gate, pre_up = t_ref[:, :n], t_ref[:, n:]
    sig = jax.nn.sigmoid(pre_gate)
    silu_v = pre_gate * sig
    cf = dot(pick_ref[...], cot_ref[...]) if packed else cot_ref[...].astype(F32)
    gp = (cf * pre_up * sig * (1.0 + pre_gate * (1.0 - sig))).astype(BF)
    up = (cf * silu_v).astype(BF)
    acted = (silu_v * pre_up).astype(BF)
    acted_ref[...] = dot(pick_ref[...], acted, ((0,), (0,))).astype(BF) if packed else acted
    gg_ref[...] = dot(x_ref[...], gp, ((0,), (0,))).astype(BF)
    ug_ref[...] = dot(x_ref[...], up, ((0,), (0,))).astype(BF)
    back_ref[...] += dot(gp, wg_ref[...], ((1,), (1,))) + dot(up, wu_ref[...], ((1,), (1,)))


def main_call(x, wg, wu, make=None, end=None):
    rows, width = x.shape
    ins, in_specs = [x], [whole(x.shape)]
    outs, out_specs, alias, scratch = [], [], {}, []
    end_steps = make_steps = 0
    if end is not None:
        part, t, pick, cot, acted, gg, ug, back = end
        packed = int(pick is not None)
        end_steps = part.steps
        for arr, spec, into in (
            (wg, part.inside(width), None),
            (wu, part.inside(width), None),
            (t, part.own(rows), None),
            (pick, None if pick is None else whole(pick.shape), None),
            (cot, part.inside(cot.shape[0]), None),
            (back, whole(back.shape), 3),
            (acted, ANY, 0),
            (gg, ANY, 1),
            (ug, ANY, 2),
        ):
            if arr is None:
                continue
            if into is not None:
                alias[len(ins)] = into
            ins.append(arr)
            in_specs.append(spec)
        outs += [jax.ShapeDtypeStruct(v, BF) for v in (cot.shape, wg.shape, wg.shape)]
        outs += [jax.ShapeDtypeStruct(back.shape, F32)]
        out_specs += [part.inside(cot.shape[0]), part.inside(width), part.inside(width), whole(back.shape)]
    if make is not None:
        make, full = make
        make_steps = make.steps
        ins += [wg, wu]
        in_specs += [make.inside(width)] * 2
        outs.append(jax.ShapeDtypeStruct((rows, full), F32))
        out_specs.append(make.own(rows))
    n_in = len(ins)

    def body(*refs):
        i, o = refs[:n_in], refs[n_in:]
        step = pl.program_id(0)
        if make is not None:

            @pl.when(step < make_steps)
            def _():
                produce_body(i[0], i[-2], i[-1], o[-1])

        if end is not None:

            @pl.when(step < end_steps)
            def _():
                finish_body(step == 0, packed, *i[: 6 + packed], *o[:4])

    return call(body, max(end_steps, make_steps), ins, in_specs, outs, out_specs, alias, scratch, 30 * MIB)


def pipeline(rows, cap, scale, tokens, hit, rank, wg, wu, cot):
    groups, per = hit.shape
    width, hidden = wg.shape
    count = jnp.sum(hit.astype(F32), axis=1)
    packed = rows < groups * cap
    first = jnp.cumsum(count) - count if packed else cap * jnp.arange(groups, dtype=F32)
    place = jnp.where(hit, first[:, None] + rank, -1.0).reshape(1, groups * per)
    row = jnp.arange(rows, dtype=F32)[:, None]
    take = (row == place).astype(BF)
    x = dot(take, tokens).astype(BF)
    pick = None
    if packed:
        slot = jnp.arange(cap, dtype=F32)[None, :]
        slot_row = jnp.where(slot < count[:, None], first[:, None] + slot, -1.0).reshape(1, groups * cap)
        pick = (row == slot_row).astype(BF)

    dp = lax.axis_index("dp")
    inner = (dp == 1) | (dp == 2)
    body, lag = (BODY, LAG) if 2 * rows > groups * cap else (LIGHT_BODY, LIGHT_LAG)
    parts = [Part(at, n) for at, n in chunks_of(hidden, body)]
    full = 2 * parts[0].n
    acted = gg = ug = None
    back = jnp.zeros((rows, width), F32)
    token = x
    p, q, b, sent, got = {}, {}, {}, {}, {}
    last = len(parts)
    lag = min(lag, last)

    def finish(j):
        nonlocal token, acted, gg, ug, back
        both = jnp.where(inner, sent.pop(j + lag), got.pop(j + lag)).astype(F32) * (1.0 / scale)
        args = (parts[j], both, pick, cot, acted, gg, ug, back)
        acted, gg, ug, back = main_call(then(x, token), wg, wu, None, args)
        token = back

    def make(j):
        p[j] = (main_call(then(x, token), wg, wu, (parts[j], full))[0] * scale).astype(HALF)

    def add(one, two):
        return (one.astype(F32) + two.astype(F32)).astype(HALF)

    def side(j):
        nonlocal token
        i = j - lag
        if i >= 0:
            total = add(q.pop(i), then(b.pop(i), token))
            sent[j] = token = jnp.where(inner, total, p[j]) if j < last else total
        else:
            sent[j] = then(p[j], token)
        got[j] = lax.ppermute(sent[j], "dp", SIDE)

    for j in range(min(lag - 1, last)):
        make(j)
        side(j)
    for j in range(lag - 1, min(4, last)):
        make(j)
    for k in range(last + lag):
        if k < last:
            q[k] = token = add(p.pop(k), then(got[k], token))
            b[k] = lax.ppermute(q[k], "dp", MID)
        if k + lag - 1 < last + lag:
            side(k + lag - 1)
        for j in (2 * k + 4, 2 * k + 5):
            if j < last:
                make(j)
        if k >= lag:
            finish(k - lag)
    own = dot(take, back.astype(BF), ((0,), (0,))).astype(BF)
    return acted, gg, ug, own


def local(tokens, expert_ids, w_gate, w_up, cotangent):
    rows, width = tokens.shape
    experts = lax.axis_size("expert")
    cap = min(rows, 4 * rows // experts)
    wg, wu, cot = w_gate[0], w_up[0], cotangent[0]
    me = lax.axis_index("expert")
    bound = 6.0 * 0.109375 * width * lax.axis_size("dp")
    scale = 2.0 ** math.floor(math.log2(65000.0 / bound))
    ids = jnp.pad(expert_ids.astype(BF), ((0, 0), (0, 126)))
    held = gather_expert(jnp.concatenate([tokens, ids], axis=1))
    all_tokens, all_ids = held[:, :, :width], held[:, :, width : width + 2]
    hit = jnp.any(all_ids == me.astype(BF), axis=2)
    before = (jnp.arange(rows)[:, None] < jnp.arange(rows)[None, :]).astype(BF)
    rank = dot(hit.astype(BF), before)
    slots = experts * cap
    sizes = sorted({slots * part // 16 for part in (6, 8, 16)}, reverse=True)
    filled = jnp.sum(hit.astype(jnp.int32))
    which = jnp.sum((filled <= jnp.array(sizes[1:], jnp.int32)).astype(jnp.int32))
    acted, gg, ug, own = lax.switch(
        which,
        [functools.partial(pipeline, size, cap, scale) for size in sizes],
        all_tokens.reshape(experts * rows, width),
        hit,
        rank,
        wg,
        wu,
        cot,
    )
    part = scatter_expert(own.reshape(experts, rows, width))
    if lax.axis_size("section") == 2:
        total = part.astype(F32) + swap(part, "section", 1).astype(F32)
    else:
        total = lax.psum(part.astype(F32), "section")
    return acted[None], total.astype(BF), gg[None], ug[None]


def solution(mesh):
    placed = (
        P("expert", "dp"),
        P("expert", None),
        P("expert", "dp", "section"),
        P("expert", "dp", "section"),
        P("expert", None, "section"),
    )
    return jax.shard_map(
        local,
        mesh=mesh,
        in_specs=placed,
        out_specs=(
            P("expert", None, "section"),
            P("expert", "dp"),
            P("expert", "dp", "section"),
            P("expert", "dp", "section"),
        ),
        check_vma=False,
    )
```

```python
import functools
import math

import jax
import jax.numpy as jnp
from jax import lax
from jax.experimental import pallas as pl
from jax.experimental.pallas import tpu as pltpu
from jax.sharding import PartitionSpec as P

BF, HALF, F32 = jnp.bfloat16, jnp.float16, jnp.float32
BODY, LAG = 256, 3
LIGHT_BODY, LIGHT_LAG = 512, 2
SIDE, MID = [(0, 1), (1, 0), (2, 3), (3, 2)], [(1, 2), (2, 1)]
MIB = 1024 * 1024


def dot(a, b, dims=((1,), (0,))):
    return lax.dot_general(a, b, (dims, ((), ())), preferred_element_type=F32)


def then(value, after):
    return lax.optimization_barrier((value, after))[0]


def swap(value, axis, stride):
    n = lax.axis_size(axis)
    return lax.ppermute(value, axis, [(i, i ^ stride) for i in range(n)])


def gather_expert(value):
    n = lax.axis_size("expert")
    me = lax.axis_index("expert")
    held, stage, stride = value, 0, n // 2
    while stride >= 1:
        other = swap(held, "expert", stride)
        low = (me & stride) == 0
        held = jnp.stack([jnp.where(low, held, other), jnp.where(low, other, held)], axis=stage)
        stage, stride = stage + 1, stride // 2
    return held.reshape((n,) + value.shape)


def scatter_expert(mine, others):
    n = lax.axis_size("expert")
    me = lax.axis_index("expert")
    value = mine + swap(others, "expert", 1).astype(F32)
    stride = 2
    while stride < n:
        value = value.reshape((-1, 2) + value.shape[1:])
        low = (me & stride) == 0
        keep = jnp.where(low, value[:, 0], value[:, 1])
        send = jnp.where(low, value[:, 1], value[:, 0]).astype(BF)
        value = keep + swap(send, "expert", stride).astype(F32)
        stride *= 2
    return value.reshape(value.shape[-2:]).astype(BF)


def chunks_of(total, body):
    body = min(body, total // 2)
    sizes = [body] * (total // body) + ([total % body] if total % body else [])
    return [(sum(sizes[:i]), n) for i, n in enumerate(sizes)]


ANY = pl.BlockSpec(memory_space=pl.ANY)


def whole(shape):
    return pl.BlockSpec(shape, lambda i: (0,) * len(shape))


class Part:
    def __init__(self, at, n):
        self.at, self.n, self.wide = at, n, n if n % 256 else 256
        self.steps = n // self.wide

    def inside(self, height):
        first, steps = self.at // self.wide, self.steps
        return pl.BlockSpec((height, self.wide), lambda i: (0, first + jnp.minimum(i, steps - 1)))

    def own(self, height):
        steps = self.steps
        return pl.BlockSpec((height, 2 * self.wide), lambda i: (0, jnp.minimum(i, steps - 1)))


def call(body, steps, ins, in_specs, outs, out_specs, alias, scratch, vmem):
    return pl.pallas_call(
        body,
        grid=(steps,),
        in_specs=in_specs,
        out_specs=out_specs,
        out_shape=outs,
        scratch_shapes=scratch,
        input_output_aliases=alias,
        compiler_params=pltpu.CompilerParams(vmem_limit_bytes=vmem),
        cost_estimate=pl.CostEstimate(flops=1, bytes_accessed=1, transcendentals=0),
    )(*ins)


def produce_body(x_ref, wg_ref, wu_ref, p_ref):
    n = wg_ref.shape[1]
    p_ref[:, :n] = dot(x_ref[...], wg_ref[...])
    p_ref[:, n:] = dot(x_ref[...], wu_ref[...])


def finish_body(first, packed, x_ref, wg_ref, wu_ref, t_ref, *refs):
    n = wg_ref.shape[1]
    pick_ref = refs[0] if packed else None
    cot_ref, back_in = refs[packed : packed + 2]
    acted_ref, gg_ref, ug_ref, back_ref = refs[-4:]

    @pl.when(first)
    def _():
        back_ref[...] = back_in[...]

    pre_gate, pre_up = t_ref[:, :n], t_ref[:, n:]
    sig = jax.nn.sigmoid(pre_gate)
    silu_v = pre_gate * sig
    cf = dot(pick_ref[...], cot_ref[...]) if packed else cot_ref[...].astype(F32)
    gp = (cf * pre_up * sig * (1.0 + pre_gate * (1.0 - sig))).astype(BF)
    up = (cf * silu_v).astype(BF)
    acted = (silu_v * pre_up).astype(BF)
    acted_ref[...] = dot(pick_ref[...], acted, ((0,), (0,))).astype(BF) if packed else acted
    gg_ref[...] = dot(x_ref[...], gp, ((0,), (0,))).astype(BF)
    ug_ref[...] = dot(x_ref[...], up, ((0,), (0,))).astype(BF)
    back_ref[...] += dot(gp, wg_ref[...], ((1,), (1,))) + dot(up, wu_ref[...], ((1,), (1,)))


def main_call(x, wg, wu, make=None, end=None):
    rows, width = x.shape
    ins, in_specs = [x], [whole(x.shape)]
    outs, out_specs, alias, scratch = [], [], {}, []
    end_steps = make_steps = 0
    if end is not None:
        part, t, pick, cot, acted, gg, ug, back = end
        packed = int(pick is not None)
        end_steps = part.steps
        for arr, spec, into in (
            (wg, part.inside(width), None),
            (wu, part.inside(width), None),
            (t, part.own(rows), None),
            (pick, None if pick is None else whole(pick.shape), None),
            (cot, part.inside(cot.shape[0]), None),
            (back, whole(back.shape), 3),
            (acted, ANY, 0),
            (gg, ANY, 1),
            (ug, ANY, 2),
        ):
            if arr is None:
                continue
            if into is not None:
                alias[len(ins)] = into
            ins.append(arr)
            in_specs.append(spec)
        outs += [jax.ShapeDtypeStruct(v, BF) for v in (cot.shape, wg.shape, wg.shape)]
        outs += [jax.ShapeDtypeStruct(back.shape, F32)]
        out_specs += [part.inside(cot.shape[0]), part.inside(width), part.inside(width), whole(back.shape)]
    if make is not None:
        make, full = make
        make_steps = make.steps
        ins += [wg, wu]
        in_specs += [make.inside(width)] * 2
        outs.append(jax.ShapeDtypeStruct((rows, full), F32))
        out_specs.append(make.own(rows))
    n_in = len(ins)

    def body(*refs):
        i, o = refs[:n_in], refs[n_in:]
        step = pl.program_id(0)
        if make is not None:

            @pl.when(step < make_steps)
            def _():
                produce_body(i[0], i[-2], i[-1], o[-1])

        if end is not None:

            @pl.when(step < end_steps)
            def _():
                finish_body(step == 0, packed, *i[: 6 + packed], *o[:4])

    return call(body, max(end_steps, make_steps), ins, in_specs, outs, out_specs, alias, scratch, 30 * MIB)


def pipeline(rows, cap, scale, tokens, hit, rank, wg, wu, cot):
    groups, per = hit.shape
    width, hidden = wg.shape
    count = jnp.sum(hit.astype(F32), axis=1)
    packed = rows < groups * cap
    first = jnp.cumsum(count) - count if packed else cap * jnp.arange(groups, dtype=F32)
    place = jnp.where(hit, first[:, None] + rank, -1.0).reshape(1, groups * per)
    row = jnp.arange(rows, dtype=F32)[:, None]
    take = (row == place).astype(BF)
    x = dot(take, tokens).astype(BF)
    pick = None
    if packed:
        slot = jnp.arange(cap, dtype=F32)[None, :]
        slot_row = jnp.where(slot < count[:, None], first[:, None] + slot, -1.0).reshape(1, groups * cap)
        pick = (row == slot_row).astype(BF)

    dp = lax.axis_index("dp")
    inner = (dp == 1) | (dp == 2)
    body, lag = (BODY, LAG) if 2 * rows > groups * cap else (LIGHT_BODY, LIGHT_LAG)
    parts = [Part(at, n) for at, n in chunks_of(hidden, body)]
    full = 2 * parts[0].n
    acted = gg = ug = None
    back = jnp.zeros((rows, width), F32)
    token = x
    p, q, b, sent, got = {}, {}, {}, {}, {}
    last = len(parts)
    lag = min(lag, last)

    def finish(j):
        nonlocal token, acted, gg, ug, back
        both = jnp.where(inner, sent.pop(j + lag), got.pop(j + lag)).astype(F32) * (1.0 / scale)
        args = (parts[j], both, pick, cot, acted, gg, ug, back)
        acted, gg, ug, back = main_call(then(x, token), wg, wu, None, args)
        token = back

    def make(j):
        p[j] = (main_call(then(x, token), wg, wu, (parts[j], full))[0] * scale).astype(HALF)

    def add(one, two):
        return (one.astype(F32) + two.astype(F32)).astype(HALF)

    def side(j):
        nonlocal token
        i = j - lag
        if i >= 0:
            total = add(q.pop(i), then(b.pop(i), token))
            sent[j] = token = jnp.where(inner, total, p[j]) if j < last else total
        else:
            sent[j] = then(p[j], token)
        got[j] = lax.ppermute(sent[j], "dp", SIDE)

    for j in range(min(lag - 1, last)):
        make(j)
        side(j)
    for j in range(lag - 1, min(4, last)):
        make(j)
    for k in range(last + lag):
        if k < last:
            q[k] = token = add(p.pop(k), then(got[k], token))
            b[k] = lax.ppermute(q[k], "dp", MID)
        if k + lag - 1 < last + lag:
            side(k + lag - 1)
        for j in (2 * k + 4, 2 * k + 5):
            if j < last:
                make(j)
        if k >= lag:
            finish(k - lag)
    by_bit = take.reshape(rows, -1, 2, per)
    bit = lax.axis_index("expert") & 1
    low = back.astype(BF)
    mine, others = [
        dot(lax.dynamic_index_in_dim(by_bit, which, 2, False).reshape(rows, -1), low, ((0,), (0,)))
        for which in (bit, 1 - bit)
    ]
    return acted, gg, ug, mine, others.astype(BF)


def local(tokens, expert_ids, w_gate, w_up, cotangent):
    rows, width = tokens.shape
    experts = lax.axis_size("expert")
    cap = min(rows, 4 * rows // experts)
    wg, wu, cot = w_gate[0], w_up[0], cotangent[0]
    me = lax.axis_index("expert")
    bound = 6.0 * 0.109375 * width * lax.axis_size("dp")
    scale = 2.0 ** math.floor(math.log2(65000.0 / bound))
    ids = jnp.pad(expert_ids.astype(BF), ((0, 0), (0, 126)))
    held = gather_expert(jnp.concatenate([tokens, ids], axis=1))
    all_tokens, all_ids = held[:, :, :width], held[:, :, width : width + 2]
    hit = jnp.any(all_ids == me.astype(BF), axis=2)
    before = (jnp.arange(rows)[:, None] < jnp.arange(rows)[None, :]).astype(BF)
    rank = dot(hit.astype(BF), before)
    slots = experts * cap
    sizes = sorted({slots * part // 16 for part in (6, 8, 16)}, reverse=True)
    filled = jnp.sum(hit.astype(jnp.int32))
    which = jnp.sum((filled <= jnp.array(sizes[1:], jnp.int32)).astype(jnp.int32))
    acted, gg, ug, mine, others = lax.switch(
        which,
        [functools.partial(pipeline, size, cap, scale) for size in sizes],
        all_tokens.reshape(experts * rows, width),
        hit,
        rank,
        wg,
        wu,
        cot,
    )
    halves = (experts // 2, rows, width)
    part = scatter_expert(mine.reshape(halves), others.reshape(halves))
    if lax.axis_size("section") == 2:
        total = part.astype(F32) + swap(part, "section", 1).astype(F32)
    else:
        total = lax.psum(part.astype(F32), "section")
    return acted[None], total.astype(BF), gg[None], ug[None]


def solution(mesh):
    placed = (
        P("expert", "dp"),
        P("expert", None),
        P("expert", "dp", "section"),
        P("expert", "dp", "section"),
        P("expert", None, "section"),
    )
    return jax.shard_map(
        local,
        mesh=mesh,
        in_specs=placed,
        out_specs=(
            P("expert", None, "section"),
            P("expert", "dp"),
            P("expert", "dp", "section"),
            P("expert", "dp", "section"),
        ),
        check_vma=False,
    )
```

```python
import functools
import math

import jax
import jax.numpy as jnp
from jax import lax
from jax.experimental import pallas as pl
from jax.experimental.pallas import tpu as pltpu
from jax.sharding import PartitionSpec as P

BF, HALF, F32 = jnp.bfloat16, jnp.float16, jnp.float32
BODY, LAG = 256, 3
LIGHT_BODY, LIGHT_LAG = 512, 2
SIDE, MID = [(0, 1), (1, 0), (2, 3), (3, 2)], [(1, 2), (2, 1)]
MIB = 1024 * 1024


def dot(a, b, dims=((1,), (0,))):
    return lax.dot_general(a, b, (dims, ((), ())), preferred_element_type=F32)


def then(value, after):
    return lax.optimization_barrier((value, after))[0]


def swap(value, axis, stride):
    n = lax.axis_size(axis)
    return lax.ppermute(value, axis, [(i, i ^ stride) for i in range(n)])


def gather_expert(value):
    n = lax.axis_size("expert")
    me = lax.axis_index("expert")
    held, stage, stride = value, 0, n // 2
    while stride >= 1:
        other = swap(held, "expert", stride)
        low = (me & stride) == 0
        held = jnp.stack([jnp.where(low, held, other), jnp.where(low, other, held)], axis=stage)
        stage, stride = stage + 1, stride // 2
    return held.reshape((n,) + value.shape)


def scatter_expert(mine, others):
    n = lax.axis_size("expert")
    me = lax.axis_index("expert")
    value = mine + swap(others, "expert", 1).astype(F32)
    stride = 2
    while stride < n:
        value = value.reshape((-1, 2) + value.shape[1:])
        low = (me & stride) == 0
        keep = jnp.where(low, value[:, 0], value[:, 1])
        send = jnp.where(low, value[:, 1], value[:, 0]).astype(BF)
        value = keep + swap(send, "expert", stride).astype(F32)
        stride *= 2
    return value.reshape(value.shape[-2:]).astype(BF)


def chunks_of(total, body):
    body = min(body, total // 2)
    sizes = [body] * (total // body) + ([total % body] if total % body else [])
    return [(sum(sizes[:i]), n) for i, n in enumerate(sizes)]


ANY = pl.BlockSpec(memory_space=pl.ANY)


def whole(shape):
    return pl.BlockSpec(shape, lambda i: (0,) * len(shape))


class Part:
    def __init__(self, at, n):
        self.at, self.n, self.wide = at, n, n if n % 256 else 256
        self.steps = n // self.wide

    def inside(self, height):
        first, steps = self.at // self.wide, self.steps
        return pl.BlockSpec((height, self.wide), lambda i: (0, first + jnp.minimum(i, steps - 1)))

    def own(self, height):
        steps = self.steps
        return pl.BlockSpec((height, 2 * self.wide), lambda i: (0, jnp.minimum(i, steps - 1)))


def call(body, steps, ins, in_specs, outs, out_specs, alias, scratch, vmem):
    return pl.pallas_call(
        body,
        grid=(steps,),
        in_specs=in_specs,
        out_specs=out_specs,
        out_shape=outs,
        scratch_shapes=scratch,
        input_output_aliases=alias,
        compiler_params=pltpu.CompilerParams(vmem_limit_bytes=vmem),
        cost_estimate=pl.CostEstimate(flops=1, bytes_accessed=1, transcendentals=0),
    )(*ins)


def produce_body(x_ref, wg_ref, wu_ref, p_ref):
    n = wg_ref.shape[1]
    p_ref[:, :n] = dot(x_ref[...], wg_ref[...])
    p_ref[:, n:] = dot(x_ref[...], wu_ref[...])


def finish_body(first, packed, x_ref, wg_ref, wu_ref, t_ref, *refs):
    n = wg_ref.shape[1]
    pick_ref = refs[0] if packed else None
    cot_ref, back_in = refs[packed : packed + 2]
    acted_ref, gg_ref, ug_ref, back_ref = refs[-4:]

    @pl.when(first)
    def _():
        back_ref[...] = back_in[...]

    pre_gate, pre_up = t_ref[:, :n], t_ref[:, n:]
    sig = jax.nn.sigmoid(pre_gate)
    silu_v = pre_gate * sig
    cf = dot(pick_ref[...], cot_ref[...]) if packed else cot_ref[...].astype(F32)
    gp = (cf * pre_up * sig * (1.0 + pre_gate * (1.0 - sig))).astype(BF)
    up = (cf * silu_v).astype(BF)
    acted = (silu_v * pre_up).astype(BF)
    acted_ref[...] = dot(pick_ref[...], acted, ((0,), (0,))).astype(BF) if packed else acted
    gg_ref[...] = dot(x_ref[...], gp, ((0,), (0,))).astype(BF)
    ug_ref[...] = dot(x_ref[...], up, ((0,), (0,))).astype(BF)
    back_ref[...] += dot(gp, wg_ref[...], ((1,), (1,))) + dot(up, wu_ref[...], ((1,), (1,)))


def main_call(x, wg, wu, make=None, end=None):
    rows, width = x.shape
    ins, in_specs = [x], [whole(x.shape)]
    outs, out_specs, alias, scratch = [], [], {}, []
    end_steps = make_steps = 0
    if end is not None:
        part, t, pick, cot, acted, gg, ug, back = end
        packed = int(pick is not None)
        end_steps = part.steps
        for arr, spec, into in (
            (wg, part.inside(width), None),
            (wu, part.inside(width), None),
            (t, part.own(rows), None),
            (pick, None if pick is None else whole(pick.shape), None),
            (cot, part.inside(cot.shape[0]), None),
            (back, whole(back.shape), 3),
            (acted, ANY, 0),
            (gg, ANY, 1),
            (ug, ANY, 2),
        ):
            if arr is None:
                continue
            if into is not None:
                alias[len(ins)] = into
            ins.append(arr)
            in_specs.append(spec)
        outs += [jax.ShapeDtypeStruct(v, BF) for v in (cot.shape, wg.shape, wg.shape)]
        outs += [jax.ShapeDtypeStruct(back.shape, F32)]
        out_specs += [part.inside(cot.shape[0]), part.inside(width), part.inside(width), whole(back.shape)]
    if make is not None:
        make, full = make
        make_steps = make.steps
        ins += [wg, wu]
        in_specs += [make.inside(width)] * 2
        outs.append(jax.ShapeDtypeStruct((rows, full), F32))
        out_specs.append(make.own(rows))
    n_in = len(ins)

    def body(*refs):
        i, o = refs[:n_in], refs[n_in:]
        step = pl.program_id(0)
        if make is not None:

            @pl.when(step < make_steps)
            def _():
                produce_body(i[0], i[-2], i[-1], o[-1])

        if end is not None:

            @pl.when(step < end_steps)
            def _():
                finish_body(step == 0, packed, *i[: 6 + packed], *o[:4])

    return call(body, max(end_steps, make_steps), ins, in_specs, outs, out_specs, alias, scratch, 30 * MIB)


def pipeline(rows, cap, scale, tokens, hit, rank, wg, wu, cot):
    groups, per = hit.shape
    width, hidden = wg.shape
    count = jnp.sum(hit.astype(F32), axis=1)
    packed = rows < groups * cap
    first = jnp.cumsum(count) - count if packed else cap * jnp.arange(groups, dtype=F32)
    place = jnp.where(hit, first[:, None] + rank, -1.0).reshape(1, groups * per)
    row = jnp.arange(rows, dtype=F32)[:, None]
    take = (row == place).astype(BF)
    x = dot(take, tokens).astype(BF)
    pick = None
    if packed:
        slot = jnp.arange(cap, dtype=F32)[None, :]
        slot_row = jnp.where(slot < count[:, None], first[:, None] + slot, -1.0).reshape(1, groups * cap)
        pick = (row == slot_row).astype(BF)

    dp = lax.axis_index("dp")
    inner = (dp == 1) | (dp == 2)
    body, lag = (BODY, LAG) if 2 * rows > groups * cap else (LIGHT_BODY, LIGHT_LAG)
    parts = [Part(at, n) for at, n in chunks_of(hidden, body)]
    full = 2 * parts[0].n
    acted = gg = ug = None
    back = jnp.zeros((rows, width), F32)
    token = x
    p, q, b, sent, got = {}, {}, {}, {}, {}
    last = len(parts)
    lag = min(lag, last)

    def finish(j):
        nonlocal token, acted, gg, ug, back
        both = jnp.where(inner, sent.pop(j + lag), got.pop(j + lag)).astype(F32) * (1.0 / scale)
        args = (parts[j], both, pick, cot, acted, gg, ug, back)
        acted, gg, ug, back = main_call(then(x, token), wg, wu, None, args)
        token = back

    def make(j):
        p[j] = (main_call(then(x, token), wg, wu, (parts[j], full))[0] * scale).astype(HALF)

    def add(one, two):
        return (one.astype(F32) + two.astype(F32)).astype(HALF)

    def side(j):
        nonlocal token
        i = j - lag
        if i >= 0:
            total = add(q.pop(i), then(b.pop(i), token))
            sent[j] = token = jnp.where(inner, total, p[j]) if j < last else total
        else:
            sent[j] = then(p[j], token)
        got[j] = lax.ppermute(sent[j], "dp", SIDE)

    for j in range(min(lag - 1, last)):
        make(j)
        side(j)
    for j in range(lag - 1, min(4, last)):
        make(j)
    for k in range(last + lag):
        if k < last:
            q[k] = token = add(p.pop(k), then(got[k], token))
            b[k] = lax.ppermute(q[k], "dp", MID)
        if k + lag - 1 < last + lag:
            side(k + lag - 1)
        for j in (2 * k + 4, 2 * k + 5):
            if j < last:
                make(j)
        if k >= lag:
            finish(k - lag)
    by_bit = take.reshape(rows, -1, 2, per)
    bit = lax.axis_index("expert") & 1
    low = back.astype(BF)
    mine, others = [
        dot(lax.dynamic_index_in_dim(by_bit, which, 2, False).reshape(rows, -1), low, ((0,), (0,)))
        for which in (bit, 1 - bit)
    ]
    return acted, gg, ug, mine, others.astype(BF)


def local(tokens, expert_ids, w_gate, w_up, cotangent):
    rows, width = tokens.shape
    experts = lax.axis_size("expert")
    cap = min(rows, 4 * rows // experts)
    wg, wu, cot = w_gate[0], w_up[0], cotangent[0]
    me = lax.axis_index("expert")
    bound = 6.0 * 0.109375 * width * lax.axis_size("dp")
    scale = 2.0 ** math.floor(math.log2(65000.0 / bound))
    ids = jnp.pad(expert_ids.astype(BF), ((0, 0), (0, 126)))
    held = gather_expert(jnp.concatenate([tokens, ids], axis=1))
    all_tokens, all_ids = held[:, :, :width], held[:, :, width : width + 2]
    hit = jnp.any(all_ids == me.astype(BF), axis=2)
    before = (jnp.arange(rows)[:, None] < jnp.arange(rows)[None, :]).astype(BF)
    rank = dot(hit.astype(BF), before)
    slots = experts * cap
    sizes = [slots, slots * 6 // 16, slots // 2]
    filled = jnp.sum(hit.astype(jnp.int32))
    which = jnp.where(filled <= sizes[1], 1, jnp.where(filled <= sizes[2], 2, 0))
    acted, gg, ug, mine, others = lax.switch(
        which,
        [functools.partial(pipeline, size, cap, scale) for size in sizes],
        all_tokens.reshape(experts * rows, width),
        hit,
        rank,
        wg,
        wu,
        cot,
    )
    halves = (experts // 2, rows, width)
    part = scatter_expert(mine.reshape(halves), others.reshape(halves))
    if lax.axis_size("section") == 2:
        total = part.astype(F32) + swap(part, "section", 1).astype(F32)
    else:
        total = lax.psum(part.astype(F32), "section")
    return acted[None], total.astype(BF), gg[None], ug[None]


def solution(mesh):
    placed = (
        P("expert", "dp"),
        P("expert", None),
        P("expert", "dp", "section"),
        P("expert", "dp", "section"),
        P("expert", None, "section"),
    )
    return jax.shard_map(
        local,
        mesh=mesh,
        in_specs=placed,
        out_specs=(
            P("expert", None, "section"),
            P("expert", "dp"),
            P("expert", "dp", "section"),
            P("expert", "dp", "section"),
        ),
        check_vma=False,
    )
```

```python
import functools
import math

import jax
import jax.numpy as jnp
from jax import lax
from jax.experimental import pallas as pl
from jax.experimental.pallas import tpu as pltpu
from jax.sharding import PartitionSpec as P

BF, HALF, F32 = jnp.bfloat16, jnp.float16, jnp.float32
BODY, LAG = 256, 3
LIGHT_BODY, LIGHT_LAG = 512, 2
SIDE, MID = [(0, 1), (1, 0), (2, 3), (3, 2)], [(1, 2), (2, 1)]
MIB = 1024 * 1024


def dot(a, b, dims=((1,), (0,))):
    return lax.dot_general(a, b, (dims, ((), ())), preferred_element_type=F32)


def then(value, after):
    return lax.optimization_barrier((value, after))[0]


def swap(value, axis, stride):
    n = lax.axis_size(axis)
    return lax.ppermute(value, axis, [(i, i ^ stride) for i in range(n)])


def gather_expert(value):
    n = lax.axis_size("expert")
    me = lax.axis_index("expert")
    held, stage, stride = value, 0, n // 2
    while stride >= 1:
        other = swap(held, "expert", stride)
        low = (me & stride) == 0
        held = jnp.stack([jnp.where(low, held, other), jnp.where(low, other, held)], axis=stage)
        stage, stride = stage + 1, stride // 2
    return held.reshape((n,) + value.shape)


def scatter_expert(mine, others):
    n = lax.axis_size("expert")
    me = lax.axis_index("expert")
    value = mine + swap(others, "expert", 1).astype(F32)
    stride = 2
    while stride < n:
        value = value.reshape((-1, 2) + value.shape[1:])
        low = (me & stride) == 0
        keep = jnp.where(low, value[:, 0], value[:, 1])
        send = jnp.where(low, value[:, 1], value[:, 0]).astype(BF)
        value = keep + swap(send, "expert", stride).astype(F32)
        stride *= 2
    return value.reshape(value.shape[-2:]).astype(BF)


def chunks_of(total, body):
    body = min(body, total // 2)
    sizes = [body] * (total // body) + ([total % body] if total % body else [])
    return [(sum(sizes[:i]), n) for i, n in enumerate(sizes)]


ANY = pl.BlockSpec(memory_space=pl.ANY)


def whole(shape):
    return pl.BlockSpec(shape, lambda i: (0,) * len(shape))


class Part:
    def __init__(self, at, n):
        self.at, self.n, self.wide = at, n, n if n % 256 else 256
        self.steps = n // self.wide

    def inside(self, height):
        first, steps = self.at // self.wide, self.steps
        return pl.BlockSpec((height, self.wide), lambda i: (0, first + jnp.minimum(i, steps - 1)))

    def own(self, height):
        steps = self.steps
        return pl.BlockSpec((height, 2 * self.wide), lambda i: (0, jnp.minimum(i, steps - 1)))


def call(body, steps, ins, in_specs, outs, out_specs, alias, scratch, vmem):
    return pl.pallas_call(
        body,
        grid=(steps,),
        in_specs=in_specs,
        out_specs=out_specs,
        out_shape=outs,
        scratch_shapes=scratch,
        input_output_aliases=alias,
        compiler_params=pltpu.CompilerParams(vmem_limit_bytes=vmem),
        cost_estimate=pl.CostEstimate(flops=1, bytes_accessed=1, transcendentals=0),
    )(*ins)


def produce_body(x_ref, wg_ref, wu_ref, p_ref):
    n = wg_ref.shape[1]
    p_ref[:, :n] = dot(x_ref[...], wg_ref[...])
    p_ref[:, n:] = dot(x_ref[...], wu_ref[...])


def finish_body(first, packed, x_ref, wg_ref, wu_ref, t_ref, *refs):
    n = wg_ref.shape[1]
    pick_ref = refs[0] if packed else None
    cot_ref, back_in = refs[packed : packed + 2]
    acted_ref, gg_ref, ug_ref, back_ref = refs[-4:]

    @pl.when(first)
    def _():
        back_ref[...] = back_in[...]

    pre_gate, pre_up = t_ref[:, :n], t_ref[:, n:]
    sig = jax.nn.sigmoid(pre_gate)
    silu_v = pre_gate * sig
    cf = dot(pick_ref[...], cot_ref[...]) if packed else cot_ref[...].astype(F32)
    gp = (cf * pre_up * sig * (1.0 + pre_gate * (1.0 - sig))).astype(BF)
    up = (cf * silu_v).astype(BF)
    acted = (silu_v * pre_up).astype(BF)
    acted_ref[...] = dot(pick_ref[...], acted, ((0,), (0,))).astype(BF) if packed else acted
    gg_ref[...] = dot(x_ref[...], gp, ((0,), (0,))).astype(BF)
    ug_ref[...] = dot(x_ref[...], up, ((0,), (0,))).astype(BF)
    back_ref[...] += dot(gp, wg_ref[...], ((1,), (1,))) + dot(up, wu_ref[...], ((1,), (1,)))


def main_call(x, wg, wu, make=None, end=None):
    rows, width = x.shape
    ins, in_specs = [x], [whole(x.shape)]
    outs, out_specs, alias, scratch = [], [], {}, []
    end_steps = make_steps = 0
    if end is not None:
        part, t, pick, cot, acted, gg, ug, back = end
        packed = int(pick is not None)
        end_steps = part.steps
        for arr, spec, into in (
            (wg, part.inside(width), None),
            (wu, part.inside(width), None),
            (t, part.own(rows), None),
            (pick, None if pick is None else whole(pick.shape), None),
            (cot, part.inside(cot.shape[0]), None),
            (back, whole(back.shape), 3),
            (acted, ANY, 0),
            (gg, ANY, 1),
            (ug, ANY, 2),
        ):
            if arr is None:
                continue
            if into is not None:
                alias[len(ins)] = into
            ins.append(arr)
            in_specs.append(spec)
        outs += [jax.ShapeDtypeStruct(v, BF) for v in (cot.shape, wg.shape, wg.shape)]
        outs += [jax.ShapeDtypeStruct(back.shape, F32)]
        out_specs += [part.inside(cot.shape[0]), part.inside(width), part.inside(width), whole(back.shape)]
    if make is not None:
        make, full = make
        make_steps = make.steps
        ins += [wg, wu]
        in_specs += [make.inside(width)] * 2
        outs.append(jax.ShapeDtypeStruct((rows, full), F32))
        out_specs.append(make.own(rows))
    n_in = len(ins)

    def body(*refs):
        i, o = refs[:n_in], refs[n_in:]
        step = pl.program_id(0)
        if make is not None:

            @pl.when(step < make_steps)
            def _():
                produce_body(i[0], i[-2], i[-1], o[-1])

        if end is not None:

            @pl.when(step < end_steps)
            def _():
                finish_body(step == 0, packed, *i[: 6 + packed], *o[:4])

    return call(body, max(end_steps, make_steps), ins, in_specs, outs, out_specs, alias, scratch, 30 * MIB)


def pipeline(rows, cap, scale, tokens, hit, rank, wg, wu, cot):
    groups, per = hit.shape
    width, hidden = wg.shape
    count = jnp.sum(hit.astype(F32), axis=1)
    packed = rows < groups * cap
    first = jnp.cumsum(count) - count if packed else cap * jnp.arange(groups, dtype=F32)
    place = jnp.where(hit, first[:, None] + rank, -1.0).reshape(1, groups * per)
    row = jnp.arange(rows, dtype=F32)[:, None]
    take = (row == place).astype(BF)
    x = dot(take, tokens).astype(BF)
    pick = None
    if packed:
        slot = jnp.arange(cap, dtype=F32)[None, :]
        slot_row = jnp.where(slot < count[:, None], first[:, None] + slot, -1.0).reshape(1, groups * cap)
        pick = (row == slot_row).astype(BF)

    dp = lax.axis_index("dp")
    inner = (dp == 1) | (dp == 2)
    body, lag = (BODY, LAG) if 2 * rows > groups * cap else (LIGHT_BODY, LIGHT_LAG)
    parts = [Part(at, n) for at, n in chunks_of(hidden, body)]
    full = 2 * parts[0].n
    acted = gg = ug = None
    back = jnp.zeros((rows, width), F32)
    token = x
    p, q, b, sent, got = {}, {}, {}, {}, {}
    last = len(parts)
    lag = min(lag, last)

    def finish(j):
        nonlocal token, acted, gg, ug, back
        both = jnp.where(inner, sent.pop(j + lag), got.pop(j + lag)).astype(F32) * (1.0 / scale)
        args = (parts[j], both, pick, cot, acted, gg, ug, back)
        acted, gg, ug, back = main_call(then(x, token), wg, wu, None, args)
        token = back

    def make(j):
        p[j] = (main_call(then(x, token), wg, wu, (parts[j], full))[0] * scale).astype(HALF)

    def add(one, two):
        return (one.astype(F32) + two.astype(F32)).astype(HALF)

    def side(j):
        nonlocal token
        i = j - lag
        if i >= 0:
            total = add(q.pop(i), then(b.pop(i), token))
            sent[j] = token = jnp.where(inner, total, p[j]) if j < last else total
        else:
            sent[j] = then(p[j], token)
        got[j] = lax.ppermute(sent[j], "dp", SIDE)

    for j in range(min(lag - 1, last)):
        make(j)
        side(j)
    for j in range(lag - 1, min(4, last)):
        make(j)
    for k in range(last + lag):
        if k < last:
            q[k] = token = add(p.pop(k), then(got[k], token))
            b[k] = lax.ppermute(q[k], "dp", MID)
        if k + lag - 1 < last + lag:
            side(k + lag - 1)
        for j in (2 * k + 4, 2 * k + 5):
            if j < last:
                make(j)
        if k >= lag:
            finish(k - lag)
    by_bit = take.reshape(rows, -1, 2, per)
    bit = lax.axis_index("expert") & 1
    low = back.astype(BF)
    mine, others = [
        dot(lax.dynamic_index_in_dim(by_bit, which, 2, False).reshape(rows, -1), low, ((0,), (0,)))
        for which in (bit, 1 - bit)
    ]
    return acted, gg, ug, mine, others.astype(BF)


def local(tokens, expert_ids, w_gate, w_up, cotangent):
    rows, width = tokens.shape
    experts = lax.axis_size("expert")
    cap = min(rows, 4 * rows // experts)
    wg, wu, cot = w_gate[0], w_up[0], cotangent[0]
    me = lax.axis_index("expert")
    bound = 6.0 * 0.109375 * width * lax.axis_size("dp")
    scale = 2.0 ** math.floor(math.log2(65000.0 / bound))
    ids = jnp.pad(expert_ids.astype(BF), ((0, 0), (0, 126)))
    held = gather_expert(jnp.concatenate([tokens, ids], axis=1))
    all_tokens, all_ids = held[:, :, :width], held[:, :, width : width + 2]
    hit = jnp.any(all_ids == me.astype(BF), axis=2)
    before = (jnp.arange(rows)[:, None] < jnp.arange(rows)[None, :]).astype(BF)
    rank = dot(hit.astype(BF), before)
    slots = experts * cap
    sizes = [slots, slots * 12 // 32, slots * 15 // 32]
    filled = jnp.sum(hit.astype(jnp.int32))
    which = jnp.where(filled <= sizes[1], 1, jnp.where(filled <= sizes[2], 2, 0))
    acted, gg, ug, mine, others = lax.switch(
        which,
        [functools.partial(pipeline, size, cap, scale) for size in sizes],
        all_tokens.reshape(experts * rows, width),
        hit,
        rank,
        wg,
        wu,
        cot,
    )
    halves = (experts // 2, rows, width)
    part = scatter_expert(mine.reshape(halves), others.reshape(halves))
    if lax.axis_size("section") == 2:
        total = part.astype(F32) + swap(part, "section", 1).astype(F32)
    else:
        total = lax.psum(part.astype(F32), "section")
    return acted[None], total.astype(BF), gg[None], ug[None]


def solution(mesh):
    placed = (
        P("expert", "dp"),
        P("expert", None),
        P("expert", "dp", "section"),
        P("expert", "dp", "section"),
        P("expert", None, "section"),
    )
    return jax.shard_map(
        local,
        mesh=mesh,
        in_specs=placed,
        out_specs=(
            P("expert", None, "section"),
            P("expert", "dp"),
            P("expert", "dp", "section"),
            P("expert", "dp", "section"),
        ),
        check_vma=False,
    )
```
